1024 devices in a mesh: expert: 16 (over z), dp: 64 (over y, x, core).
Axes of the slice: x: 4, y: 8, z: 16, core: 2. Of those that a mesh axis runs over, the one named last changes fastest.
Arguments:
- tokens: bfloat16 [2560, 4096], P('dp', 'expert'), may hold values from -6 to 6
- expert_ids: int32 [2560, 8], P('dp'), may hold values from 0 to 63, all different within a row; in each aligned block of 40 rows (0 to 39, 40 to 79, ...) at most 7 rows name the same one
- gate_probs: float32 [2560, 8], P('dp'), may hold values from 0.1 to 1
- cotangent: bfloat16 [2560, 4096], P('dp', 'expert'), may hold values from -6 to 6
- w_gate: bfloat16 [64, 1024, 4096], P('dp', None, 'expert'), may hold values from -0.09375 to 0.09375
- w_up: bfloat16 [64, 1024, 4096], P('dp', None, 'expert'), may hold values from -0.09375 to 0.09375
- w_down: bfloat16 [64, 1024, 4096], P('dp', None, 'expert'), may hold values from -0.1875 to 0.1875
Outputs:
- mixed: bfloat16 [2560, 4096], P('dp', 'expert')
- token_grad: bfloat16 [2560, 4096], P('dp', 'expert')
- gate_grad: bfloat16 [64, 1024, 4096], P('dp', None, 'expert')
- up_grad: bfloat16 [64, 1024, 4096], P('dp', None, 'expert')
- down_grad: bfloat16 [64, 1024, 4096], P('dp', None, 'expert')
The draws below stay inside these ranges and needn't reach their ends.
Inputs may be any that keep to these rules, and one draw needn't show every extreme that they name: `expert_ids`: each token names 8 different experts. Among the 40 tokens of one index of dp at most 7 name any one expert, and in some such block one expert is named by exactly 7 of them.
All inputs are finite; a program needn't handle non-finite values.
Results may differ from the reference program's by a relative error of at most 0.03.
Values may be sent and summed in bfloat16 or wider, within the bound.
A program may use at most 32 MiB of HBM per device.

```python
import math
import jax
import jax.numpy as jnp
import numpy as np
from jax import lax

D = 4096
FF = 1024
TOP = 8
TOK_DP = 40
EXPERTS = 64
CAP = 7
TOKENS = 2560
N_EXPERT = 16
N_DP = 64


def steps_of(key, shape, split, low, largest):
    def one(position, blocks):
        heights = jax.random.uniform(jax.random.fold_in(jax.random.fold_in(key, 6), position), (blocks,), jnp.float32, low / len(split), largest / len(split))
        return jnp.repeat(jnp.exp(heights), shape[position] // blocks).reshape((-1,) + (1,) * (len(shape) - position - 1))

    level = one(*split[0])
    for cut in split[1:]:
        level = level * one(*cut)
    return level


def assign_block(rng, own, number, rows, number_of, top, reach, slope):
    ranking = jax.random.permutation(rng, number_of)
    packed, ordinary = shares(number_of, rows * top, reach, slope, True), shares(number_of, rows * top, reach, slope, False)
    places = jnp.arange(number_of)

    def named(tallies, turn):
        used = int((tallies > 0).sum())
        fixed = max(1, used // 4)
        shifted = fixed + (places - fixed + turn * (used - fixed)) % max(1, number_of - fixed)
        return jnp.zeros((number_of,), jnp.int32).at[ranking[jnp.where(places < fixed, places, shifted)]].set(jnp.asarray(tallies, jnp.int32))

    tallies = jnp.where(number % 4 == 0, named(packed, number // 4), named(ordinary, number - number // 4 - 1))
    mixed = jax.random.permutation(jax.random.fold_in(own, 3), number_of)
    donor, taker = mixed[0:number_of // 2 * 2:2], mixed[1:number_of // 2 * 2:2]
    slack = jnp.minimum(tallies[donor] - 1, reach - tallies[taker]) // 2
    slack = jnp.where((donor == ranking[0]) | (taker == ranking[0]) | (tallies[taker] == 0), 0, jnp.maximum(slack, 0))
    shifted = jax.random.randint(jax.random.fold_in(own, 4), (number_of // 2,), 0, 1 << 20) % (slack + 1)
    tallies = tallies.at[donor].add(-shifted).at[taker].add(shifted)
    items = jnp.searchsorted(jnp.cumsum(tallies), jnp.arange(rows * top), side="right").astype(jnp.int32)
    grid = items.reshape(top, rows).T
    grid = grid[jax.random.permutation(jax.random.fold_in(own, 1), rows)]
    turn = jax.random.randint(jax.random.fold_in(own, 2), (rows, 1), 0, top)
    return jnp.take_along_axis(grid, (jnp.arange(top)[None, :] + turn) % top, axis=1)


def shares(amount, total, most, slope, full):
    loads = [(1 << 20) // math.isqrt(standing ** slope) + 1 for standing in range(1, amount + 1)]
    largest = most if full else min(most, max(-(-total // amount), total * loads[0] // sum(loads)))
    least = 1 if total - largest >= amount - 1 else 0
    holding, surplus = [largest] + [least] * (amount - 1), total - largest - least * (amount - 1)
    while surplus > 0:
        movable = [i for i in range(1, amount) if holding[i] < largest] or [i for i in range(1, amount) if holding[i] < most]
        pool, left = sum([loads[i] for i in movable]), surplus
        for i in movable:
            more = min(most - holding[i], max(1, left * loads[i] // pool), surplus)
            holding[i] = holding[i] + more
            surplus = surplus - more
    return np.array(holding)


def gaussian(key, dims, scale, bound, shards=(), held_as=jnp.bfloat16):
    array = jax.random.normal(key, dims, jnp.float32) * scale
    if len(shards) > 0:
        array = steps_of(key, dims, shards, -0.22, 0.18) * array
    return jnp.clip(array, min=-bound, max=bound).astype(held_as)


def setup_inputs(seed: int = 0) -> dict:
    splits = jax.random.split(jax.random.key(seed), 8)
    tokens = gaussian(splits[0], (TOKENS, D), 1.0, 6.0, ((0, 64), (1, 16)))
    expert_ids_keys = jax.random.split(jax.random.fold_in(splits[1], 1), TOKENS // TOK_DP)
    expert_ids_turns = jax.random.permutation(jax.random.fold_in(splits[1], 3), TOKENS // TOK_DP)
    expert_ids = jax.vmap(lambda own, number: assign_block(jax.random.fold_in(splits[1], 2), own, number, TOK_DP, EXPERTS, TOP, CAP, 2))(expert_ids_keys, expert_ids_turns).reshape((TOKENS, TOP))
    gate_probs = jnp.clip(0.1 + 0.9 * jax.random.uniform(splits[2], (TOKENS, TOP), jnp.float32) ** steps_of(splits[2], (TOKENS, TOP), ((0, 64),), -0.2, 0.2), 0.1, 1.0)
    cotangent = gaussian(splits[3], (TOKENS, D), 1.0, 6.0, ((0, 64), (1, 16)))
    w_gate = gaussian(splits[4], (EXPERTS, FF, D), D ** -0.5, 0.09375, ((0, 64), (2, 16)))
    w_up = gaussian(splits[5], (EXPERTS, FF, D), D ** -0.5, 0.09375, ((0, 64), (2, 16)))
    w_down = gaussian(splits[6], (EXPERTS, FF, D), FF ** -0.5, 0.1875, ((0, 64), (2, 16)))
    return dict(tokens=tokens, expert_ids=expert_ids, gate_probs=gate_probs, cotangent=cotangent, w_gate=w_gate, w_up=w_up, w_down=w_down)


def slot_rows(expert_ids):
    onehot = (expert_ids[:, :, None] == jnp.arange(EXPERTS, dtype=jnp.int32)[None, None, :]).astype(jnp.int32)
    per_token = jnp.sum(onehot, axis=1).reshape(N_DP, TOK_DP, EXPERTS)
    earlier = (jnp.cumsum(per_token, axis=1) - per_token).reshape(TOKENS, EXPERTS)
    slot = jnp.sum(onehot * earlier[:, None, :], axis=2)
    block = (jnp.arange(TOKENS, dtype=jnp.int32) // TOK_DP)[:, None]
    return (block * CAP + slot).astype(jnp.int32)


def block_total(parts):
    rounded = lax.optimization_barrier(parts.astype(jnp.bfloat16))
    return jnp.sum(rounded.astype(jnp.float32), axis=0)


def feature_sum(rows, weight):
    count = rows.shape[0]
    slice_width = D // N_EXPERT
    row_blocks = rows.astype(jnp.float32).reshape(count, N_EXPERT, slice_width)
    weight_blocks = weight.astype(jnp.float32).reshape(FF, N_EXPERT, slice_width)
    parts = jnp.einsum("rbs,fbs->brf", row_blocks, weight_blocks, precision=lax.Precision.HIGHEST)
    return block_total(parts)


def expert_pass(inputs):
    xg, dg, wg, wu, wd = inputs
    down_rows = (((0,), (0,)), ((), ()))
    gate_pre = feature_sum(xg, wg)
    up_pre = feature_sum(xg, wu)
    hidden_grad = feature_sum(dg, wd)
    sigmoid_gate = jax.nn.sigmoid(gate_pre)
    active = gate_pre * sigmoid_gate
    hidden = (active * up_pre).astype(jnp.bfloat16)
    gate_delta = (hidden_grad * up_pre * sigmoid_gate * (1.0 + gate_pre * (1.0 - sigmoid_gate))).astype(jnp.bfloat16)
    up_delta = (hidden_grad * active).astype(jnp.bfloat16)
    out_rows = jnp.dot(hidden, wd, preferred_element_type=jnp.float32).astype(jnp.bfloat16)
    back_rows = (jnp.dot(gate_delta, wg, preferred_element_type=jnp.float32) + jnp.dot(up_delta, wu, preferred_element_type=jnp.float32)).astype(jnp.bfloat16)
    down_grad = lax.dot_general(hidden, dg, down_rows, preferred_element_type=jnp.float32).astype(jnp.bfloat16)
    gate_grad = lax.dot_general(gate_delta, xg, down_rows, preferred_element_type=jnp.float32).astype(jnp.bfloat16)
    up_grad = lax.dot_general(up_delta, xg, down_rows, preferred_element_type=jnp.float32).astype(jnp.bfloat16)
    return out_rows, back_rows, gate_grad, up_grad, down_grad


def reference(tokens, expert_ids, gate_probs, cotangent, w_gate, w_up, w_down):
    row = slot_rows(expert_ids)
    rows_total = N_DP * CAP
    spread = jnp.broadcast_to(tokens[:, None, :], (TOKENS, TOP, D))
    xrows = jnp.zeros((EXPERTS, rows_total, D), jnp.bfloat16).at[expert_ids, row].set(spread)
    scaled = (gate_probs[:, :, None] * cotangent[:, None, :].astype(jnp.float32)).astype(jnp.bfloat16)
    drows = jnp.zeros((EXPERTS, rows_total, D), jnp.bfloat16).at[expert_ids, row].set(scaled)
    out_rows, back_rows, gate_grad, up_grad, down_grad = lax.map(expert_pass, (xrows, drows, w_gate, w_up, w_down))
    picked = out_rows[expert_ids, row].astype(jnp.float32)
    mixed = jnp.sum(gate_probs[:, :, None] * picked, axis=1).astype(jnp.bfloat16)
    token_grad = jnp.sum(back_rows[expert_ids, row].astype(jnp.float32), axis=1).astype(jnp.bfloat16)
    return mixed, token_grad, gate_grad, up_grad, down_grad
```

```python
import functools

import jax
import jax.numpy as jnp
from jax import lax
from jax.experimental import pallas as pl
from jax.experimental.pallas import tpu as pltpu
from jax.sharding import PartitionSpec as P

SLOTS = 8
PAIR = 2 * SLOTS
MESH = pl.DeviceIdType.MESH


def matmul(a, b, contract):
    return lax.dot_general(a, b, ((contract[0:1], contract[1:2]), ((), ())), preferred_element_type=jnp.float32)


def plan(n_z, n_dp):
    cores = 2 if n_dp >= 4 else 1
    width = 4 if n_dp >= 64 else 2
    height = n_dp // (cores * width)
    low = n_z // width
    return cores, width, height, low, n_dp // n_z


def kernel(
    n_z, n_dp, ids_ref, probs_ref, tok_ref, cot_ref, gate_hbm, up_hbm, down_hbm,
    mixed_ref, tgrad_ref, ggrad_hbm, ugrad_hbm, dgrad_hbm,
    wts, grads, route, sbuf, inbuf, obuf, rbuf, xall, dall, part, landed, held,
    w_sem, g_sem, in_send, in_recv, out_send, out_recv, rs_send, rs_recv, ag_send, ag_recv,
):
    cores, width, height, low, per = plan(n_z, n_dp)
    rows = per * SLOTS
    span = per * PAIR
    half, cut = n_z // 2, rows // 2
    n_tok, top = ids_ref.shape
    z = lax.axis_index("expert")
    g = lax.axis_index("dp")
    y, x, core = g // (width * cores), (g // cores) % width, g % cores
    z_right, z_left = (z + 1) % n_z, (z + n_z - 1) % n_z

    def partner(o, i, sign):
        dy = o // width + low * (i // cores)
        dx, dc = o % width, i % cores
        py = (y + sign * dy + height) % height
        px = (x + sign * dx + width) % width
        pc = (core + sign * dc + cores) % cores
        return (py * width + px) * cores + pc

    loads = [
        pltpu.make_async_copy(src.at[0], wts.at[n], w_sem.at[n])
        for n, src in enumerate((gate_hbm, up_hbm, down_hbm))
    ]
    for load in loads:
        load.start()

    barrier = pltpu.get_barrier_semaphore()

    @pl.loop(1, n_dp)
    def _(step):
        pl.semaphore_signal(barrier, inc=1, device_id={"dp": (g + step) % n_dp}, device_id_type=MESH)

    for near in (z_right, z_left):
        pl.semaphore_signal(barrier, inc=1, device_id={"expert": near}, device_id_type=MESH)

    lane = lax.broadcasted_iota(jnp.int32, (1, n_z * span), 1)
    o_of, i_of, r_of = lane // span, (lane % span) // PAIR, lane % PAIR
    ly = (y + o_of // width + low * (i_of // cores)) % height
    lx = (x + o_of % width) % width
    lc = (core + i_of % cores) % cores
    expert_of = (ly * width + lx) * cores + lc
    ids, probs = ids_ref[...], probs_ref[...]
    named = jnp.zeros((n_tok, n_z * span), jnp.float32)
    weight = jnp.zeros((n_tok, n_z * span), jnp.float32)
    for k in range(top):
        hit = ids[:, k : k + 1] == expert_of
        named = jnp.where(hit, 1.0, named)
        weight = jnp.where(hit, probs[:, k : k + 1], weight)
    before = (
        lax.broadcasted_iota(jnp.int32, (n_tok, n_tok), 1) < lax.broadcasted_iota(jnp.int32, (n_tok, n_tok), 0)
    ).astype(jnp.float32)
    slot = matmul(before, named, (1, 0))
    chosen = jnp.where(slot == (r_of % SLOTS).astype(jnp.float32), named, 0.0)
    first = r_of < SLOTS
    plain = jnp.where(first, chosen, 0.0)
    scale = jnp.where(first, 0.0, chosen * weight)
    high = scale.astype(jnp.bfloat16).astype(jnp.float32)
    mid = (scale - high).astype(jnp.bfloat16).astype(jnp.float32)
    route[...] = jnp.concatenate([plain, high, mid, scale - high - mid], axis=0).astype(jnp.bfloat16)
    tok, cot = tok_ref[...].astype(jnp.float32), cot_ref[...].astype(jnp.float32)
    values = jnp.concatenate([tok, cot, cot, cot], axis=0).astype(jnp.bfloat16)
    sbuf[...] = matmul(route[...], values, (0, 0)).astype(jnp.bfloat16)

    pl.semaphore_wait(barrier, n_dp + 1)

    def exchange(src, dst, send_sem, recv_sem, o, sign):
        for i in range(per):
            at = pl.ds(pl.multiple_of(o * span + i * PAIR, PAIR), PAIR)

            def remote():
                pltpu.make_async_remote_copy(
                    src_ref=src.at[at],
                    dst_ref=dst.at[at],
                    send_sem=send_sem,
                    recv_sem=recv_sem,
                    device_id={"dp": partner(o, i, sign)},
                    device_id_type=MESH,
                ).start()

            if i:
                remote()
            else:

                @pl.when(o == 0)
                def _():
                    pltpu.make_async_copy(src.at[at], dst.at[at], recv_sem).start()

                @pl.when(o != 0)
                def _():
                    remote()

    def wait_rows(ref, first_row, count, sem):
        view = ref.at[pl.ds(first_row, count)]
        pltpu.make_async_copy(view, view, sem).wait()

    def send_in(o):
        exchange(sbuf, inbuf, in_send, in_recv.at[o], o, 1)

    far = (z + half) % n_z
    send_in(far)

    @pl.loop(1, half)
    def _(s):
        send_in((z + half - s) % n_z)
        send_in((z + half + s) % n_z)

    send_in(z)
    for load in loads:
        load.wait()

    def partials(chunks):
        xs, ds = [], []
        for o in chunks:
            at = pl.multiple_of(o * span, span)
            wait_rows(inbuf, at, span, in_recv.at[o])
            both = inbuf[pl.ds(at, span), :].astype(jnp.float32).reshape(per, 2, SLOTS, -1)
            to = pl.ds(pl.multiple_of(o * rows, rows), rows)
            xs.append(both[:, 0].reshape(rows, -1).astype(jnp.bfloat16))
            ds.append(both[:, 1].reshape(rows, -1).astype(jnp.bfloat16))
            xall[to, :] = xs[-1]
            dall[to, :] = ds[-1]
        xrows = jnp.concatenate(xs, axis=0) if len(xs) > 1 else xs[0]
        drows = jnp.concatenate(ds, axis=0) if len(ds) > 1 else ds[0]
        for a, lhs in enumerate((xrows, xrows, drows)):
            product = matmul(lhs, wts[a], (1, 1)).astype(jnp.bfloat16)
            for n, o in enumerate(chunks):
                part[a, o] = product[n * rows : (n + 1) * rows]

    sides = (z_right, z_left)

    def rs_copy(d, s, a, o, at=None):
        src, dst = part.at[a, o], landed.at[d, s, a]
        if at is not None:
            src, dst = src.at[at], dst.at[at]
        return pltpu.make_async_remote_copy(
            src_ref=src,
            dst_ref=dst,
            send_sem=rs_send.at[d, s, a],
            recv_sem=rs_recv.at[d, s, a],
            device_id={"expert": sides[d]},
            device_id_type=MESH,
        )

    def ag_copy(d, s, a, o, at=None):
        src, dst = held.at[a, o], held.at[a, o]
        if at is not None:
            src, dst = src.at[at], dst.at[at]
        return pltpu.make_async_remote_copy(
            src_ref=src,
            dst_ref=dst,
            send_sem=ag_send.at[d, s, a],
            recv_sem=ag_recv.at[d, s, a],
            device_id={"expert": sides[d]},
            device_id_type=MESH,
        )

    halves = (pl.ds(0, cut), pl.ds(cut, cut))

    partials([far])
    for a in range(3):
        for d in range(2):
            rs_copy(d, 0, a, far, halves[d]).start()

    def ends(s):
        return (z + half - s) % n_z, (z + half + s) % n_z

    partials(ends(1))
    for a in range(3):
        for d in range(2):
            o = ends(1)[d]
            rs_copy(d, 0, a, o, halves[d]).wait_recv()
            at = halves[d]
            part[a, o, at, :] = (
                part[a, o, at, :].astype(jnp.float32) + landed[d, 0, a, at, :].astype(jnp.float32)
            ).astype(jnp.bfloat16)
            rs_copy(d, 1, a, o).start()

    @pl.loop(2, half)
    def _(s):
        chunks = ends(s)
        partials(chunks)
        for a in range(3):
            for d in range(2):
                o = chunks[d]
                rs_copy(d, s - 1, a, o).wait_recv()
                part[a, o] = (
                    part[a, o].astype(jnp.float32) + landed[d, s - 1, a].astype(jnp.float32)
                ).astype(jnp.bfloat16)
                rs_copy(d, s, a, o).start()

    partials([z])
    sums = []
    for a in range(3):
        for d in range(2):
            rs_copy(d, half - 1, a, z).wait_recv()
        sums.append(
            part[a, z].astype(jnp.float32)
            + landed[0, half - 1, a].astype(jnp.float32)
            + landed[1, half - 1, a].astype(jnp.float32)
        )
    gate, up, hgrad = sums
    sig = jax.nn.sigmoid(gate)
    active = gate * sig
    held[0, z] = (hgrad * up * sig * (1.0 + gate * (1.0 - sig))).astype(jnp.bfloat16)
    held[1, z] = (hgrad * active).astype(jnp.bfloat16)
    held[2, z] = (active * up).astype(jnp.bfloat16)
    for a in range(3):
        for d in range(2):
            ag_copy(d, 1, a, z).start()

    def outward(chunks):
        lhs = [
            jnp.concatenate([held[a, o] for o in chunks], axis=0) if len(chunks) > 1 else held[a, chunks[0]]
            for a in range(3)
        ]
        back = matmul(lhs[0], wts[0], (1, 0)) + matmul(lhs[1], wts[1], (1, 0))
        out = matmul(lhs[2], wts[2], (1, 0))
        for n, o in enumerate(chunks):
            mine = slice(n * rows, (n + 1) * rows)
            both = jnp.stack(
                [back[mine].reshape(per, SLOTS, -1), out[mine].reshape(per, SLOTS, -1)], axis=1
            ).reshape(span, -1)
            obuf[pl.ds(pl.multiple_of(o * span, span), span), :] = both.astype(jnp.bfloat16)
            exchange(obuf, rbuf, out_send, out_recv, o, -1)

    outward([z])

    @pl.loop(1, half - 1)
    def _(s):
        chunks = ((z - s + n_z) % n_z, (z + s) % n_z)
        for a in range(3):
            for d in range(2):
                ag_copy(d, s, a, chunks[d]).wait_recv()
                ag_copy(d, s + 1, a, chunks[d]).start()
        outward(chunks)

    last = ((z - (half - 1) + n_z) % n_z, (z + half - 1) % n_z)
    for a in range(3):
        for d in range(2):
            ag_copy(d, half - 1, a, last[d]).wait_recv()
            ag_copy(d, half, a, last[d], halves[d]).start()
    outward(last)
    for a in range(3):
        for d in range(2):
            ag_copy(d, half, a, far, halves[d]).wait_recv()
    outward([far])

    stores = []
    for a, dst in enumerate((ggrad_hbm, ugrad_hbm, dgrad_hbm)):
        whole = held[a].reshape(n_z * rows, -1)
        rhs = (dall if a == 2 else xall)[...]
        grads[a] = matmul(whole, rhs, (0, 0)).astype(jnp.bfloat16)
        stores.append(pltpu.make_async_copy(grads.at[a], dst.at[0], g_sem.at[a]))
        stores[-1].start()

    wait_rows(rbuf, 0, n_z * span, out_recv)
    total = matmul(route[...], rbuf[...], (1, 0))
    tgrad_ref[...] = total[:n_tok].astype(jnp.bfloat16)
    mixed_ref[...] = (total[n_tok : 2 * n_tok] + total[2 * n_tok : 3 * n_tok] + total[3 * n_tok :]).astype(
        jnp.bfloat16
    )

    wait_rows(sbuf, 0, n_z * span - PAIR, in_send)
    wait_rows(obuf, 0, n_z * span - PAIR, out_send)
    for a in range(3):
        for d in range(2):
            rs_copy(d, 0, a, far, halves[d]).wait_send()
            ag_copy(d, half, a, far, halves[d]).wait_send()

    @pl.loop(1, half)
    def _(s):
        for a in range(3):
            for d in range(2):
                rs_copy(d, s, a, z).wait_send()
                ag_copy(d, s, a, z).wait_send()

    for store in stores:
        store.wait()


def shards(n_z, n_dp, tokens, expert_ids, gate_probs, cotangent, w_gate, w_up, w_down):
    n_tok, feats = tokens.shape
    ff = w_gate.shape[1]
    rows = n_dp // n_z * SLOTS
    both = n_dp * PAIR
    half = n_z // 2
    bf16 = jnp.bfloat16
    vmem = pl.BlockSpec(memory_space=pltpu.VMEM)
    anywhere = pl.BlockSpec(memory_space=pl.ANY)
    act = jax.ShapeDtypeStruct((n_tok, feats), bf16)
    grad = jax.ShapeDtypeStruct((1, ff, feats), bf16)
    dma = pltpu.SemaphoreType.DMA
    return pl.pallas_call(
        functools.partial(kernel, n_z, n_dp),
        out_shape=(act, act, grad, grad, grad),
        in_specs=[vmem] * 4 + [anywhere] * 3,
        out_specs=(vmem, vmem, anywhere, anywhere, anywhere),
        scratch_shapes=[
            pltpu.VMEM((3, ff, feats), bf16),
            pltpu.VMEM((3, ff, feats), bf16),
            pltpu.VMEM((4 * n_tok, both), bf16),
            pltpu.VMEM((both, feats), bf16),
            pltpu.VMEM((both, feats), bf16),
            pltpu.VMEM((both, feats), bf16),
            pltpu.VMEM((both, feats), bf16),
            pltpu.VMEM((n_z * rows, feats), bf16),
            pltpu.VMEM((n_z * rows, feats), bf16),
            pltpu.VMEM((3, n_z, rows, ff), bf16),
            pltpu.VMEM((2, half, 3, rows, ff), bf16),
            pltpu.VMEM((3, n_z, rows, ff), bf16),
            dma((3,)),
            dma((3,)),
            dma,
            dma((n_z,)),
            dma,
            dma,
            dma((2, half, 3)),
            dma((2, half, 3)),
            dma((2, half + 1, 3)),
            dma((2, half + 1, 3)),
        ],
        compiler_params=pltpu.CompilerParams(
            collective_id=0, has_side_effects=True, vmem_limit_bytes=56 * 1024 * 1024
        ),
        name="experts",
    )(expert_ids, gate_probs, tokens, cotangent, w_gate, w_up, w_down)


def solution(mesh):
    n_z, n_dp = mesh.shape["expert"], mesh.shape["dp"]
    split = P("dp", "expert")
    weight = P("dp", None, "expert")
    return jax.shard_map(
        functools.partial(shards, n_z, n_dp),
        mesh=mesh,
        in_specs=(split, P("dp", None), P("dp", None), split, weight, weight, weight),
        out_specs=(split, split, weight, weight, weight),
        check_vma=False,
    )
```

```python
import functools

import jax
import jax.numpy as jnp
from jax import lax
from jax.experimental import pallas as pl
from jax.experimental.pallas import tpu as pltpu
from jax.sharding import PartitionSpec as P

SLOTS = 8
USED = 7
CUTS = 4
PAIR = 2 * SLOTS
MESH = pl.DeviceIdType.MESH


def matmul(a, b, contract):
    return lax.dot_general(a, b, ((contract[0:1], contract[1:2]), ((), ())), preferred_element_type=jnp.float32)


def plan(n_z, n_dp):
    cores = 2 if n_dp >= 4 else 1
    width = 4 if n_dp >= 64 else 2
    height = n_dp // (cores * width)
    low = n_z // width
    return cores, width, height, low, n_dp // n_z


def kernel(
    n_z, n_dp, ids_hbm, probs_hbm, tok_hbm, cot_hbm, gate_hbm, up_hbm, down_hbm,
    route, rbuf, grads,
    ids_ref, probs_ref, tok_ref, cot_ref, wts, sbuf, inbuf, obuf, xall, dall, pack, unpack, part, landed, held, hall,
    w_sem, t_sem, in_send, in_recv, out_send, out_recv, rs_send, rs_recv, ag_send, ag_recv,
):
    cores, width, height, low, per = plan(n_z, n_dp)
    rows = per * SLOTS
    span = per * PAIR
    quarter = wts.shape[1] // CUTS
    packed = CUTS * per * USED
    half, cut = n_z // 2, -(-packed // 32) * 16
    top, n_tok = ids_ref.shape
    z = lax.axis_index("expert")
    g = lax.axis_index("dp")
    y, x, core = g // (width * cores), (g // cores) % width, g % cores
    z_right, z_left = (z + 1) % n_z, (z + n_z - 1) % n_z

    def partner(o, i, sign):
        dy = o // width + low * (i // cores)
        dx, dc = o % width, i % cores
        py = (y + sign * dy + height) % height
        px = (x + sign * dx + width) % width
        pc = (core + sign * dc + cores) % cores
        return (py * width + px) * cores + pc

    loads = [
        pltpu.make_async_copy(src.at[0], wts.at[n], w_sem.at[n])
        for n, src in enumerate((gate_hbm, up_hbm, down_hbm))
    ]
    small = [
        pltpu.make_async_copy(src, dst, t_sem.at[n])
        for n, (src, dst) in enumerate(
            ((ids_hbm, ids_ref), (probs_hbm, probs_ref), (tok_hbm, tok_ref), (cot_hbm, cot_ref))
        )
    ]
    for load in small + loads:
        load.start()

    barrier = pltpu.get_barrier_semaphore()

    @pl.loop(1, n_dp)
    def _(step):
        pl.semaphore_signal(barrier, inc=1, device_id={"dp": (g + step) % n_dp}, device_id_type=MESH)

    for near in (z_right, z_left):
        pl.semaphore_signal(barrier, inc=1, device_id={"expert": near}, device_id_type=MESH)

    lane = lax.broadcasted_iota(jnp.int32, (1, n_z * span), 1)
    o_of, i_of, r_of = lane // span, (lane % span) // PAIR, lane % PAIR
    ly = (y + o_of // width + low * (i_of // cores)) % height
    lx = (x + o_of % width) % width
    lc = (core + i_of % cores) % cores
    expert_of = (ly * width + lx) * cores + lc
    for load in small:
        load.wait()
    ids, probs = ids_ref[...].T, probs_ref[...].T
    named = jnp.zeros((n_tok, n_z * span), jnp.float32)
    weight = jnp.zeros((n_tok, n_z * span), jnp.float32)
    for k in range(top):
        hit = ids[:, k : k + 1] == expert_of
        named = jnp.where(hit, 1.0, named)
        weight = jnp.where(hit, probs[:, k : k + 1], weight)
    before = (
        lax.broadcasted_iota(jnp.int32, (n_tok, n_tok), 1) < lax.broadcasted_iota(jnp.int32, (n_tok, n_tok), 0)
    ).astype(jnp.float32)
    slot = matmul(before, named, (1, 0))
    chosen = jnp.where(slot == (r_of % SLOTS).astype(jnp.float32), named, 0.0)
    first = r_of < SLOTS
    plain = jnp.where(first, chosen, 0.0)
    scale = jnp.where(first, 0.0, chosen * weight)
    high = scale.astype(jnp.bfloat16).astype(jnp.float32)
    mid = (scale - high).astype(jnp.bfloat16).astype(jnp.float32)
    route[...] = jnp.concatenate([plain, high, mid, scale - high - mid], axis=0).astype(jnp.bfloat16)

    def place(dim, shape):
        c = lax.broadcasted_iota(jnp.int32, shape, dim)
        r, i, f = c % SLOTS, (c % rows) // SLOTS, c // rows
        to = (f * per + i) * USED + r
        return ((r < USED) & (to == lax.broadcasted_iota(jnp.int32, shape, 1 - dim))).astype(jnp.float32)

    pack[...] = place(1, (packed, CUTS * rows)).astype(jnp.bfloat16)
    unpack[...] = place(0, (CUTS * rows, packed)).astype(jnp.bfloat16)

    tok, cot = tok_ref[...].astype(jnp.float32), cot_ref[...].astype(jnp.float32)
    values = jnp.concatenate([tok, cot, cot, cot], axis=0).astype(jnp.bfloat16)
    sbuf[...] = matmul(route[...], values, (0, 0)).astype(jnp.bfloat16)

    pl.semaphore_wait(barrier, n_dp + 1)

    def exchange(src, dst, send_sem, recv_sem, o, sign):
        for i in range(per):
            at = pl.ds(pl.multiple_of(o * span + i * PAIR, PAIR), PAIR)

            def remote():
                pltpu.make_async_remote_copy(
                    src_ref=src.at[at],
                    dst_ref=dst.at[at],
                    send_sem=send_sem,
                    recv_sem=recv_sem,
                    device_id={"dp": partner(o, i, sign)},
                    device_id_type=MESH,
                ).start()

            if i:
                remote()
            else:

                @pl.when(o == 0)
                def _():
                    pltpu.make_async_copy(src.at[at], dst.at[at], recv_sem).start()

                @pl.when(o != 0)
                def _():
                    remote()

    def wait_rows(ref, first_row, count, sem):
        view = ref.at[pl.ds(first_row, count)]
        pltpu.make_async_copy(view, view, sem).wait()

    def send_in(o):
        exchange(sbuf, inbuf, in_send, in_recv.at[o], o, 1)

    far = (z + half) % n_z
    send_in(far)

    @pl.loop(1, half)
    def _(s):
        send_in((z + half - s) % n_z)
        send_in((z + half + s) % n_z)

    send_in(z)
    for load in loads:
        load.wait()

    def partials(chunks):
        xs, ds = [], []
        for o in chunks:
            at = pl.multiple_of(o * span, span)
            wait_rows(inbuf, at, span, in_recv.at[o])
            both = inbuf[pl.ds(at, span), :].astype(jnp.float32).reshape(per, 2, SLOTS, -1)
            to = pl.ds(pl.multiple_of(o * rows, rows), rows)
            xs.append(both[:, 0].reshape(rows, -1).astype(jnp.bfloat16))
            ds.append(both[:, 1].reshape(rows, -1).astype(jnp.bfloat16))
            xall[to, :] = xs[-1]
            dall[to, :] = ds[-1]
        xrows = jnp.concatenate(xs, axis=0) if len(xs) > 1 else xs[0]
        drows = jnp.concatenate(ds, axis=0) if len(ds) > 1 else ds[0]
        for a, lhs in enumerate((xrows, xrows, drows)):
            product = matmul(lhs, wts[a], (1, 1)).astype(jnp.bfloat16)
            for n, o in enumerate(chunks):
                mine = product[n * rows : (n + 1) * rows]
                stacked = jnp.concatenate(
                    [mine[:, f * quarter : (f + 1) * quarter] for f in range(CUTS)], axis=0
                )
                part[a, o] = matmul(pack[...], stacked, (1, 0)).astype(jnp.bfloat16)

    sides = (z_right, z_left)

    def rs_copy(d, s, a, o, at=None):
        src, dst = part.at[a, o], landed.at[d, s, a]
        if at is not None:
            src, dst = src.at[at], dst.at[at]
        return pltpu.make_async_remote_copy(
            src_ref=src,
            dst_ref=dst,
            send_sem=rs_send.at[d, s, a],
            recv_sem=rs_recv.at[d, s, a],
            device_id={"expert": sides[d]},
            device_id_type=MESH,
        )

    def ag_copy(d, s, a, o, at=None):
        src, dst = held.at[a, o], held.at[a, o]
        if at is not None:
            src, dst = src.at[at], dst.at[at]
        return pltpu.make_async_remote_copy(
            src_ref=src,
            dst_ref=dst,
            send_sem=ag_send.at[d, s, a],
            recv_sem=ag_recv.at[d, s, a],
            device_id={"expert": sides[d]},
            device_id_type=MESH,
        )

    halves = (pl.ds(0, cut), pl.ds(cut, packed - cut))

    partials([far])
    for a in range(3):
        for d in range(2):
            rs_copy(d, 0, a, far, halves[d]).start()

    def ends(s):
        return (z + half - s) % n_z, (z + half + s) % n_z

    partials(ends(1))
    for a in range(3):
        for d in range(2):
            o = ends(1)[d]
            rs_copy(d, 0, a, o, halves[d]).wait_recv()
            at = halves[d]
            part[a, o, at, :] = (
                part[a, o, at, :].astype(jnp.float32) + landed[d, 0, a, at, :].astype(jnp.float32)
            ).astype(jnp.bfloat16)
            rs_copy(d, 1, a, o).start()

    @pl.loop(2, half)
    def _(s):
        chunks = ends(s)
        partials(chunks)
        for a in range(3):
            for d in range(2):
                o = chunks[d]
                rs_copy(d, s - 1, a, o).wait_recv()
                part[a, o] = (
                    part[a, o].astype(jnp.float32) + landed[d, s - 1, a].astype(jnp.float32)
                ).astype(jnp.bfloat16)
                rs_copy(d, s, a, o).start()

    partials([z])
    sums = []
    for a in range(3):
        for d in range(2):
            rs_copy(d, half - 1, a, z).wait_recv()
        sums.append(
            part[a, z].astype(jnp.float32)
            + landed[0, half - 1, a].astype(jnp.float32)
            + landed[1, half - 1, a].astype(jnp.float32)
        )
    gate, up, hgrad = sums
    sig = jax.nn.sigmoid(gate)
    active = gate * sig
    held[0, z] = (hgrad * up * sig * (1.0 + gate * (1.0 - sig))).astype(jnp.bfloat16)
    held[1, z] = (hgrad * active).astype(jnp.bfloat16)
    held[2, z] = (active * up).astype(jnp.bfloat16)
    for a in range(3):
        for d in range(2):
            ag_copy(d, 1, a, z).start()

    def outward(chunks):
        lhs = []
        for a in range(3):
            whole = []
            for o in chunks:
                stacked = matmul(unpack[...], held[a, o], (1, 0)).astype(jnp.bfloat16)
                whole.append(
                    jnp.concatenate([stacked[f * rows : (f + 1) * rows] for f in range(CUTS)], axis=1)
                )
                hall[a, pl.ds(pl.multiple_of(o * rows, rows), rows), :] = whole[-1]
            lhs.append(jnp.concatenate(whole, axis=0) if len(whole) > 1 else whole[0])
        back = matmul(lhs[0], wts[0], (1, 0)) + matmul(lhs[1], wts[1], (1, 0))
        out = matmul(lhs[2], wts[2], (1, 0))
        for n, o in enumerate(chunks):
            mine = slice(n * rows, (n + 1) * rows)
            both = jnp.stack(
                [back[mine].reshape(per, SLOTS, -1), out[mine].reshape(per, SLOTS, -1)], axis=1
            ).reshape(span, -1)
            obuf[pl.ds(pl.multiple_of(o * span, span), span), :] = both.astype(jnp.bfloat16)
            exchange(obuf, rbuf, out_send, out_recv, o, -1)

    outward([z])

    @pl.loop(1, half - 1)
    def _(s):
        chunks = ((z - s + n_z) % n_z, (z + s) % n_z)
        for a in range(3):
            for d in range(2):
                ag_copy(d, s, a, chunks[d]).wait_recv()
                ag_copy(d, s + 1, a, chunks[d]).start()
        outward(chunks)

    last = ((z - (half - 1) + n_z) % n_z, (z + half - 1) % n_z)
    for a in range(3):
        for d in range(2):
            ag_copy(d, half - 1, a, last[d]).wait_recv()
            ag_copy(d, half, a, last[d], halves[d]).start()
    outward(last)
    for a in range(3):
        for d in range(2):
            ag_copy(d, half, a, far, halves[d]).wait_recv()
    outward([far])

    for a in range(3):
        grads[a] = matmul(hall[a], (dall if a == 2 else xall)[...], (0, 0)).astype(jnp.bfloat16)

    wait_rows(rbuf, 0, n_z * span, out_recv)
    wait_rows(sbuf, 0, n_z * span - PAIR, in_send)
    wait_rows(obuf, 0, n_z * span - PAIR, out_send)
    for a in range(3):
        for d in range(2):
            rs_copy(d, 0, a, far, halves[d]).wait_send()
            ag_copy(d, half, a, far, halves[d]).wait_send()

    @pl.loop(1, half)
    def _(s):
        for a in range(3):
            for d in range(2):
                rs_copy(d, s, a, z).wait_send()
                ag_copy(d, s, a, z).wait_send()


def finish(route, rbuf, grads, mixed_ref, tgrad_ref, ggrad_hbm, ugrad_hbm, dgrad_hbm, sem):
    stores = [
        pltpu.make_async_copy(grads.at[a], dst.at[0], sem.at[a])
        for a, dst in enumerate((ggrad_hbm, ugrad_hbm, dgrad_hbm))
    ]
    for store in stores:
        store.start()
    n_tok = mixed_ref.shape[0]
    total = matmul(route[...], rbuf[...], (1, 0))
    tgrad_ref[...] = total[:n_tok].astype(jnp.bfloat16)
    mixed_ref[...] = (total[n_tok : 2 * n_tok] + total[2 * n_tok : 3 * n_tok] + total[3 * n_tok :]).astype(
        jnp.bfloat16
    )
    for store in stores:
        store.wait()


def shards(n_z, n_dp, tokens, expert_ids, gate_probs, cotangent, w_gate, w_up, w_down):
    n_tok, feats = tokens.shape
    ff = w_gate.shape[1]
    rows = n_dp // n_z * SLOTS
    both = n_dp * PAIR
    packed = CUTS * (n_dp // n_z) * USED
    half = n_z // 2
    bf16 = jnp.bfloat16
    vmem = pl.BlockSpec(memory_space=pltpu.VMEM)
    anywhere = pl.BlockSpec(memory_space=pltpu.HBM)
    act = jax.ShapeDtypeStruct((n_tok, feats), bf16)
    grad = jax.ShapeDtypeStruct((1, ff, feats), bf16)
    dma = pltpu.SemaphoreType.DMA
    route, rbuf, grads = pl.pallas_call(
        functools.partial(kernel, n_z, n_dp),
        out_shape=(
            pltpu.VMEM((4 * n_tok, both), bf16),
            pltpu.VMEM((both, feats), bf16),
            pltpu.VMEM((3, ff, feats), bf16),
        ),
        in_specs=[anywhere] * 7,
        out_specs=(vmem, vmem, vmem),
        scratch_shapes=[
            pltpu.VMEM(expert_ids.shape[::-1], jnp.int32),
            pltpu.VMEM(expert_ids.shape[::-1], jnp.float32),
            pltpu.VMEM((n_tok, feats), bf16),
            pltpu.VMEM((n_tok, feats), bf16),
            pltpu.VMEM((3, ff, feats), bf16),
            pltpu.VMEM((both, feats), bf16),
            pltpu.VMEM((both, feats), bf16),
            pltpu.VMEM((both, feats), bf16),
            pltpu.VMEM((n_z * rows, feats), bf16),
            pltpu.VMEM((n_z * rows, feats), bf16),
            pltpu.VMEM((packed, CUTS * rows), bf16),
            pltpu.VMEM((CUTS * rows, packed), bf16),
            pltpu.VMEM((3, n_z, packed, ff // CUTS), bf16),
            pltpu.VMEM((2, half, 3, packed, ff // CUTS), bf16),
            pltpu.VMEM((3, n_z, packed, ff // CUTS), bf16),
            pltpu.VMEM((3, n_z * rows, ff), bf16),
            dma((3,)),
            dma((4,)),
            dma,
            dma((n_z,)),
            dma,
            dma,
            dma((2, half, 3)),
            dma((2, half, 3)),
            dma((2, half + 1, 3)),
            dma((2, half + 1, 3)),
        ],
        compiler_params=pltpu.CompilerParams(
            collective_id=0, has_side_effects=True, vmem_limit_bytes=56 * 1024 * 1024
        ),
        name="experts",
    )(expert_ids.T, gate_probs.T, tokens, cotangent, w_gate, w_up, w_down)
    return pl.pallas_call(
        finish,
        out_shape=(act, act, grad, grad, grad),
        in_specs=[vmem] * 3,
        out_specs=(vmem, vmem, anywhere, anywhere, anywhere),
        scratch_shapes=[dma((3,))],
        compiler_params=pltpu.CompilerParams(vmem_limit_bytes=16 * 1024 * 1024),
        name="finish",
    )(route, rbuf, grads)


def solution(mesh):
    n_z, n_dp = mesh.shape["expert"], mesh.shape["dp"]
    split = P("dp", "expert")
    weight = P("dp", None, "expert")
    return jax.shard_map(
        functools.partial(shards, n_z, n_dp),
        mesh=mesh,
        in_specs=(split, P("dp", None), P("dp", None), split, weight, weight, weight),
        out_specs=(split, split, weight, weight, weight),
        check_vma=False,
    )
```

```python
import functools

import jax
import jax.numpy as jnp
from jax import lax
from jax.experimental import pallas as pl
from jax.experimental.pallas import tpu as pltpu
from jax.sharding import PartitionSpec as P

SLOTS = 8
USED = 7
CUTS = 4
PIECES = 5
PAIR = 2 * SLOTS
MESH = pl.DeviceIdType.MESH


def matmul(a, b, contract):
    return lax.dot_general(a, b, ((contract[0:1], contract[1:2]), ((), ())), preferred_element_type=jnp.float32)


def plan(n_z, n_dp):
    cores = 2 if n_dp >= 4 else 1
    width = 4 if n_dp >= 64 else 2
    height = n_dp // (cores * width)
    low = n_z // width
    return cores, width, height, low, n_dp // n_z


def kernel(
    n_z, n_dp, ids_hbm, probs_hbm, tok_hbm, cot_hbm, gate_hbm, up_hbm, down_hbm,
    route, rbuf, grads,
    ids_ref, probs_ref, tok_ref, cot_ref, wts, sbuf, inbuf, obuf, xall, dall, pack, unpack, part, landed, held, hall,
    w_sem, t_sem, in_send, in_recv, out_send, out_recv, rs_send, rs_recv, ag_send, ag_recv,
):
    cores, width, height, low, per = plan(n_z, n_dp)
    rows = per * SLOTS
    span = per * PAIR
    quarter = wts.shape[1] // CUTS
    packed = CUTS * per * USED
    half = n_z // 2
    size = 3 * packed // PIECES // 16 * 16
    starts = [m * size for m in range(PIECES)] + [3 * packed]
    msgs = [(m, starts[m], starts[m + 1] - starts[m]) for m in range(PIECES)]
    centre = PIECES // 2
    split = size // 32 * 16
    far_msgs = (
        msgs[:centre] + [(centre, starts[centre], split)],
        [(centre, starts[centre] + split, size - split)] + msgs[centre + 1 :],
    )
    rs_order = (msgs[centre + 1 :] + msgs[: centre + 1], msgs)
    ag_order = (msgs, msgs[centre:] + msgs[:centre])
    top, n_tok = ids_ref.shape
    z = lax.axis_index("expert")
    g = lax.axis_index("dp")
    y, x, core = g // (width * cores), (g // cores) % width, g % cores
    z_right, z_left = lax.rem(z + 1, n_z), lax.rem(z + n_z - 1, n_z)

    def partner(o, i, sign):
        dy = lax.div(o, width) + low * (i // cores)
        dx, dc = lax.rem(o, width), i % cores
        py = lax.rem(y + sign * dy + height, height)
        px = lax.rem(x + sign * dx + width, width)
        pc = lax.rem(core + sign * dc + cores, cores)
        return (py * width + px) * cores + pc

    loads = [
        pltpu.make_async_copy(src.at[0], wts.at[n], w_sem.at[n])
        for n, src in enumerate((gate_hbm, up_hbm, down_hbm))
    ]
    small = [
        pltpu.make_async_copy(src, dst, t_sem.at[n])
        for n, (src, dst) in enumerate(
            ((ids_hbm, ids_ref), (probs_hbm, probs_ref), (tok_hbm, tok_ref), (cot_hbm, cot_ref))
        )
    ]
    for load in small + loads:
        load.start()

    barrier = pltpu.get_barrier_semaphore()

    @pl.loop(1, n_dp)
    def _(step):
        pl.semaphore_signal(barrier, inc=1, device_id={"dp": lax.rem(g + step, n_dp)}, device_id_type=MESH)

    for near in (z_right, z_left):
        pl.semaphore_signal(barrier, inc=1, device_id={"expert": near}, device_id_type=MESH)

    lane = lax.broadcasted_iota(jnp.int32, (1, n_z * span), 1)
    o_of, i_of, r_of = lane // span, (lane % span) // PAIR, lane % PAIR
    ly = (y + o_of // width + low * (i_of // cores)) % height
    lx = (x + o_of % width) % width
    lc = (core + i_of % cores) % cores
    expert_of = (ly * width + lx) * cores + lc
    for load in small:
        load.wait()
    ids, probs = ids_ref[...].T, probs_ref[...].T
    named = jnp.zeros((n_tok, n_z * span), jnp.float32)
    weight = jnp.zeros((n_tok, n_z * span), jnp.float32)
    for k in range(top):
        hit = ids[:, k : k + 1] == expert_of
        named = jnp.where(hit, 1.0, named)
        weight = jnp.where(hit, probs[:, k : k + 1], weight)
    before = (
        lax.broadcasted_iota(jnp.int32, (n_tok, n_tok), 1) < lax.broadcasted_iota(jnp.int32, (n_tok, n_tok), 0)
    ).astype(jnp.float32)
    slot = matmul(before, named, (1, 0))
    chosen = jnp.where(slot == (r_of % SLOTS).astype(jnp.float32), named, 0.0)
    first = r_of < SLOTS
    plain = jnp.where(first, chosen, 0.0)
    scale = jnp.where(first, 0.0, chosen * weight)
    high = scale.astype(jnp.bfloat16).astype(jnp.float32)
    mid = (scale - high).astype(jnp.bfloat16).astype(jnp.float32)
    route[...] = jnp.concatenate([plain, high, mid, scale - high - mid], axis=0).astype(jnp.bfloat16)

    def place(dim, shape):
        c = lax.broadcasted_iota(jnp.int32, shape, dim)
        r, i, f = c % SLOTS, (c % rows) // SLOTS, c // rows
        to = (f * per + i) * USED + r
        return ((r < USED) & (to == lax.broadcasted_iota(jnp.int32, shape, 1 - dim))).astype(jnp.float32)

    pack[...] = place(1, (packed, CUTS * rows)).astype(jnp.bfloat16)
    unpack[...] = place(0, (CUTS * rows, packed)).astype(jnp.bfloat16)

    tok, cot = tok_ref[...].astype(jnp.float32), cot_ref[...].astype(jnp.float32)
    values = jnp.concatenate([tok, cot, cot, cot], axis=0).astype(jnp.bfloat16)
    sbuf[...] = matmul(route[...], values, (0, 0)).astype(jnp.bfloat16)

    pl.semaphore_wait(barrier, n_dp + 1)

    def exchange(src, dst, send_sem, recv_sem, o, sign):
        for i in range(per):
            at = pl.ds(pl.multiple_of(o * span + i * PAIR, PAIR), PAIR)

            def remote():
                pltpu.make_async_remote_copy(
                    src_ref=src.at[at],
                    dst_ref=dst.at[at],
                    send_sem=send_sem,
                    recv_sem=recv_sem,
                    device_id={"dp": partner(o, i, sign)},
                    device_id_type=MESH,
                ).start()

            if i:
                remote()
            else:

                @pl.when(o == 0)
                def _():
                    pltpu.make_async_copy(src.at[at], dst.at[at], recv_sem).start()

                @pl.when(o != 0)
                def _():
                    remote()

    def wait_rows(ref, first_row, count, sem):
        view = ref.at[pl.ds(first_row, count)]
        pltpu.make_async_copy(view, view, sem).wait()

    def send_in(o):
        exchange(sbuf, inbuf, in_send, in_recv.at[o], o, 1)

    far = (z + half) % n_z
    send_in(far)

    @pl.loop(1, half)
    def _(s):
        send_in((z + half - s) % n_z)
        send_in((z + half + s) % n_z)

    send_in(z)
    for load in loads:
        load.wait()

    def partials(chunks):
        xs, ds = [], []
        for o in chunks:
            at = pl.multiple_of(o * span, span)
            wait_rows(inbuf, at, span, in_recv.at[o])
            both = inbuf[pl.ds(at, span), :].astype(jnp.float32).reshape(per, 2, SLOTS, -1)
            to = pl.ds(pl.multiple_of(o * rows, rows), rows)
            xs.append(both[:, 0].reshape(rows, -1).astype(jnp.bfloat16))
            ds.append(both[:, 1].reshape(rows, -1).astype(jnp.bfloat16))
            xall[to, :] = xs[-1]
            dall[to, :] = ds[-1]
        xrows = jnp.concatenate(xs, axis=0) if len(xs) > 1 else xs[0]
        drows = jnp.concatenate(ds, axis=0) if len(ds) > 1 else ds[0]
        for a, lhs in enumerate((xrows, xrows, drows)):
            product = matmul(lhs, wts[a], (1, 1)).astype(jnp.bfloat16)
            for n, o in enumerate(chunks):
                mine = product[n * rows : (n + 1) * rows]
                stacked = jnp.concatenate(
                    [mine[:, f * quarter : (f + 1) * quarter] for f in range(CUTS)], axis=0
                )
                part[o, a * packed : (a + 1) * packed] = matmul(pack[...], stacked, (1, 0)).astype(jnp.bfloat16)

    sides = (z_right, z_left)

    def rs_copy(d, s, o, m, first, count):
        at = pl.ds(first, count)
        return pltpu.make_async_remote_copy(
            src_ref=part.at[o].at[at],
            dst_ref=landed.at[d, s].at[at],
            send_sem=rs_send.at[d, s, m],
            recv_sem=rs_recv.at[d, s, m],
            device_id={"expert": sides[d]},
            device_id_type=MESH,
        )

    def ag_copy(d, s, o, m, first, count):
        at = pl.ds(first, count)
        return pltpu.make_async_remote_copy(
            src_ref=held.at[o].at[at],
            dst_ref=held.at[o].at[at],
            send_sem=ag_send.at[d, s, m],
            recv_sem=ag_recv.at[d, s, m],
            device_id={"expert": sides[d]},
            device_id_type=MESH,
        )

    partials([far])
    for n in range(centre + 1):
        for d in range(2):
            rs_copy(d, 0, far, *far_msgs[d][n]).start()

    def ends(s):
        return (z + half - s) % n_z, (z + half + s) % n_z

    def add_on(d, s, o, m, first, count):
        rs_copy(d, s, o, m, first, count).wait_recv()
        at = pl.ds(first, count)
        part[o, at, :] = (
            part[o, at, :].astype(jnp.float32) + landed[d, s, at, :].astype(jnp.float32)
        ).astype(jnp.bfloat16)

    near = ends(1)
    partials(near)
    for n in range(centre):
        rs_copy(0, 1, near[0], *msgs[centre + 1 + n]).start()
        rs_copy(1, 1, near[1], *msgs[n]).start()
    for n in range(centre + 1):
        for d in range(2):
            add_on(d, 0, near[d], *far_msgs[d][n])
            rs_copy(d, 1, near[d], *msgs[far_msgs[d][n][0]]).start()

    @pl.loop(2, half)
    def _(s):
        chunks = ends(s)
        partials(chunks)
        for n in range(PIECES):
            for d in range(2):
                add_on(d, s - 1, chunks[d], *rs_order[d][n])
                rs_copy(d, s, chunks[d], *rs_order[d][n]).start()

    partials([z])

    def landed_sum(a):
        at = pl.ds(a * packed, packed)
        return (
            part[z, at, :].astype(jnp.float32)
            + landed[0, half - 1, at, :].astype(jnp.float32)
            + landed[1, half - 1, at, :].astype(jnp.float32)
        )

    def hold(a, value):
        held[z, a * packed : (a + 1) * packed] = value.astype(jnp.bfloat16)

    early = [msg for msg in msgs if msg[1] < 2 * packed]
    late = [msg for msg in msgs if msg[1] >= 2 * packed]
    ready = [msg for msg in msgs if msg[1] + msg[2] <= packed]
    for msg in early:
        for d in range(2):
            rs_copy(d, half - 1, z, *msg).wait_recv()
    gate, up = landed_sum(0), landed_sum(1)
    sig = jax.nn.sigmoid(gate)
    active = gate * sig
    hold(0, active * up)
    for msg in ready:
        for d in range(2):
            ag_copy(d, 1, z, *msg).start()
    for msg in late:
        for d in range(2):
            rs_copy(d, half - 1, z, *msg).wait_recv()
    hgrad = landed_sum(2)
    hold(1, hgrad * active)
    hold(2, hgrad * up * sig * (1.0 + gate * (1.0 - sig)))
    for n in range(PIECES):
        for d in range(2):
            if ag_order[d][n] not in ready:
                ag_copy(d, 1, z, *ag_order[d][n]).start()

    def outward(chunks):
        lhs = []
        for a in range(3):
            whole = []
            for o in chunks:
                stacked = matmul(unpack[...], held[o, a * packed : (a + 1) * packed], (1, 0)).astype(jnp.bfloat16)
                whole.append(
                    jnp.concatenate([stacked[f * rows : (f + 1) * rows] for f in range(CUTS)], axis=1)
                )
                hall[a, pl.ds(pl.multiple_of(o * rows, rows), rows), :] = whole[-1]
            lhs.append(jnp.concatenate(whole, axis=0) if len(whole) > 1 else whole[0])
        out = matmul(lhs[0], wts[2], (1, 0))
        back = matmul(lhs[1], wts[1], (1, 0)) + matmul(lhs[2], wts[0], (1, 0))
        for n, o in enumerate(chunks):
            mine = slice(n * rows, (n + 1) * rows)
            both = jnp.stack(
                [back[mine].reshape(per, SLOTS, -1), out[mine].reshape(per, SLOTS, -1)], axis=1
            ).reshape(span, -1)
            obuf[pl.ds(pl.multiple_of(o * span, span), span), :] = both.astype(jnp.bfloat16)
            exchange(obuf, rbuf, out_send, out_recv, o, -1)

    outward([z])

    @pl.loop(1, half - 1)
    def _(s):
        chunks = ((z - s + n_z) % n_z, (z + s) % n_z)
        for n in range(PIECES):
            for d in range(2):
                ag_copy(d, s, chunks[d], *ag_order[d][n]).wait_recv()
                ag_copy(d, s + 1, chunks[d], *ag_order[d][n]).start()
        outward(chunks)

    last = ((z - (half - 1) + n_z) % n_z, (z + half - 1) % n_z)
    for n in range(PIECES):
        for d in range(2):
            ag_copy(d, half - 1, last[d], *ag_order[d][n]).wait_recv()
            for part_msg in far_msgs[d]:
                if part_msg[0] == ag_order[d][n][0]:
                    ag_copy(d, half, last[d], *part_msg).start()
    outward(last)
    for d in range(2):
        for msg in far_msgs[d]:
            ag_copy(d, half, far, *msg).wait_recv()
    outward([far])

    for a in range(3):
        grads[2 - a] = matmul(hall[a], (xall if a else dall)[...], (0, 0)).astype(jnp.bfloat16)

    wait_rows(rbuf, 0, n_z * span, out_recv)
    wait_rows(sbuf, 0, n_z * span - PAIR, in_send)
    wait_rows(obuf, 0, n_z * span - PAIR, out_send)
    for d in range(2):
        for msg in far_msgs[d]:
            rs_copy(d, 0, far, *msg).wait_send()
            ag_copy(d, half, far, *msg).wait_send()

    @pl.loop(1, half)
    def _(s):
        for msg in msgs:
            for d in range(2):
                rs_copy(d, s, z, *msg).wait_send()
                ag_copy(d, s, z, *msg).wait_send()


def finish(route, rbuf, grads, mixed_ref, tgrad_ref, ggrad_hbm, ugrad_hbm, dgrad_hbm, sem):
    stores = [
        pltpu.make_async_copy(grads.at[a], dst.at[0], sem.at[a])
        for a, dst in enumerate((ggrad_hbm, ugrad_hbm, dgrad_hbm))
    ]
    for store in stores:
        store.start()
    n_tok = mixed_ref.shape[0]
    total = matmul(route[...], rbuf[...], (1, 0))
    tgrad_ref[...] = total[:n_tok].astype(jnp.bfloat16)
    mixed_ref[...] = (total[n_tok : 2 * n_tok] + total[2 * n_tok : 3 * n_tok] + total[3 * n_tok :]).astype(
        jnp.bfloat16
    )
    for store in stores:
        store.wait()


def shards(n_z, n_dp, tokens, expert_ids, gate_probs, cotangent, w_gate, w_up, w_down):
    n_tok, feats = tokens.shape
    ff = w_gate.shape[1]
    rows = n_dp // n_z * SLOTS
    both = n_dp * PAIR
    packed = CUTS * (n_dp // n_z) * USED
    half = n_z // 2
    bf16 = jnp.bfloat16
    vmem = pl.BlockSpec(memory_space=pltpu.VMEM)
    anywhere = pl.BlockSpec(memory_space=pltpu.HBM)
    act = jax.ShapeDtypeStruct((n_tok, feats), bf16)
    grad = jax.ShapeDtypeStruct((1, ff, feats), bf16)
    dma = pltpu.SemaphoreType.DMA
    route, rbuf, grads = pl.pallas_call(
        functools.partial(kernel, n_z, n_dp),
        out_shape=(
            pltpu.VMEM((4 * n_tok, both), bf16),
            pltpu.VMEM((both, feats), bf16),
            pltpu.VMEM((3, ff, feats), bf16),
        ),
        in_specs=[anywhere] * 7,
        out_specs=(vmem, vmem, vmem),
        scratch_shapes=[
            pltpu.VMEM(expert_ids.shape[::-1], jnp.int32),
            pltpu.VMEM(expert_ids.shape[::-1], jnp.float32),
            pltpu.VMEM((n_tok, feats), bf16),
            pltpu.VMEM((n_tok, feats), bf16),
            pltpu.VMEM((3, ff, feats), bf16),
            pltpu.VMEM((both, feats), bf16),
            pltpu.VMEM((both, feats), bf16),
            pltpu.VMEM((both, feats), bf16),
            pltpu.VMEM((n_z * rows, feats), bf16),
            pltpu.VMEM((n_z * rows, feats), bf16),
            pltpu.VMEM((packed, CUTS * rows), bf16),
            pltpu.VMEM((CUTS * rows, packed), bf16),
            pltpu.VMEM((n_z, 3 * packed, ff // CUTS), bf16),
            pltpu.VMEM((2, half, 3 * packed, ff // CUTS), bf16),
            pltpu.VMEM((n_z, 3 * packed, ff // CUTS), bf16),
            pltpu.VMEM((3, n_z * rows, ff), bf16),
            dma((3,)),
            dma((4,)),
            dma,
            dma((n_z,)),
            dma,
            dma,
            dma((2, half, PIECES)),
            dma((2, half, PIECES)),
            dma((2, half + 1, PIECES)),
            dma((2, half + 1, PIECES)),
        ],
        compiler_params=pltpu.CompilerParams(
            collective_id=0, has_side_effects=True, vmem_limit_bytes=56 * 1024 * 1024
        ),
        name="experts",
    )(expert_ids.T, gate_probs.T, tokens, cotangent, w_gate, w_up, w_down)
    return pl.pallas_call(
        finish,
        out_shape=(act, act, grad, grad, grad),
        in_specs=[vmem] * 3,
        out_specs=(vmem, vmem, anywhere, anywhere, anywhere),
        scratch_shapes=[dma((3,))],
        compiler_params=pltpu.CompilerParams(vmem_limit_bytes=16 * 1024 * 1024),
        name="finish",
    )(route, rbuf, grads)


def solution(mesh):
    n_z, n_dp = mesh.shape["expert"], mesh.shape["dp"]
    split = P("dp", "expert")
    weight = P("dp", None, "expert")
    return jax.shard_map(
        functools.partial(shards, n_z, n_dp),
        mesh=mesh,
        in_specs=(split, P("dp", None), P("dp", None), split, weight, weight, weight),
        out_specs=(split, split, weight, weight, weight),
        check_vma=False,
    )
```

```python
import functools

import jax
import jax.numpy as jnp
from jax import lax
from jax.experimental import pallas as pl
from jax.experimental.pallas import tpu as pltpu
from jax.sharding import PartitionSpec as P

SLOTS = 8
USED = 7
CUTS = 4
PIECES = 5
PAIR = 2 * SLOTS
MESH = pl.DeviceIdType.MESH


def matmul(a, b, contract):
    return lax.dot_general(a, b, ((contract[0:1], contract[1:2]), ((), ())), preferred_element_type=jnp.float32)


def plan(n_z, n_dp):
    cores = 2 if n_dp >= 4 else 1
    width = 4 if n_dp >= 64 else 2
    height = n_dp // (cores * width)
    low = n_z // width
    return cores, width, height, low, n_dp // n_z


def kernel(
    n_z, n_dp, ids_hbm, probs_hbm, tok_hbm, cot_hbm, gate_hbm, up_hbm, down_hbm,
    route, rbuf, grads,
    ids_ref, probs_ref, tok_ref, cot_ref, wts, sbuf, inbuf, obuf, xall, dall, pack, unpack, part, landed, held, hall,
    w_sem, t_sem, in_send, in_recv, out_send, out_recv, rs_send, rs_recv, ag_send, ag_recv,
):
    cores, width, height, low, per = plan(n_z, n_dp)
    rows = per * SLOTS
    span = per * PAIR
    quarter = wts.shape[1] // CUTS
    packed = CUTS * per * USED
    half = n_z // 2
    size = 3 * packed // PIECES // 16 * 16
    starts = [m * size for m in range(PIECES)] + [3 * packed]
    msgs = [(m, starts[m], starts[m + 1] - starts[m]) for m in range(PIECES)]
    centre = PIECES // 2
    split = size // 32 * 16
    far_msgs = (
        msgs[:centre] + [(centre, starts[centre], split)],
        [(centre, starts[centre] + split, size - split)] + msgs[centre + 1 :],
    )
    rs_order = (msgs[centre + 1 :] + msgs[: centre + 1], msgs)
    ag_order = (msgs, msgs[centre:] + msgs[:centre])
    top, n_tok = ids_ref.shape
    z = lax.axis_index("expert")
    g = lax.axis_index("dp")
    y, x, core = g // (width * cores), (g // cores) % width, g % cores
    z_right, z_left = lax.rem(z + 1, n_z), lax.rem(z + n_z - 1, n_z)

    def partner(o, i, sign):
        dy = lax.div(o, width) + low * (i // cores)
        dx, dc = lax.rem(o, width), i % cores
        py = lax.rem(y + sign * dy + height, height)
        px = lax.rem(x + sign * dx + width, width)
        pc = lax.rem(core + sign * dc + cores, cores)
        return (py * width + px) * cores + pc

    loads = [
        pltpu.make_async_copy(src.at[0], wts.at[n], w_sem.at[n])
        for n, src in enumerate((gate_hbm, up_hbm, down_hbm))
    ]
    small = [
        pltpu.make_async_copy(src, dst, t_sem.at[n])
        for n, (src, dst) in enumerate(
            ((ids_hbm, ids_ref), (probs_hbm, probs_ref), (tok_hbm, tok_ref), (cot_hbm, cot_ref))
        )
    ]
    for load in small + loads:
        load.start()

    barrier = pltpu.get_barrier_semaphore()

    @pl.loop(1, n_dp)
    def _(step):
        pl.semaphore_signal(barrier, inc=1, device_id={"dp": lax.rem(g + step, n_dp)}, device_id_type=MESH)

    for near in (z_right, z_left):
        pl.semaphore_signal(barrier, inc=1, device_id={"expert": near}, device_id_type=MESH)

    lane = lax.broadcasted_iota(jnp.int32, (1, n_z * span), 1)
    o_of, i_of, r_of = lane // span, (lane % span) // PAIR, lane % PAIR
    ly = (y + o_of // width + low * (i_of // cores)) % height
    lx = (x + o_of % width) % width
    lc = (core + i_of % cores) % cores
    expert_of = (ly * width + lx) * cores + lc
    for load in small:
        load.wait()
    ids, probs = ids_ref[...].T, probs_ref[...].T
    named = jnp.zeros((n_tok, n_z * span), jnp.float32)
    weight = jnp.zeros((n_tok, n_z * span), jnp.float32)
    for k in range(top):
        hit = ids[:, k : k + 1] == expert_of
        named = jnp.where(hit, 1.0, named)
        weight = jnp.where(hit, probs[:, k : k + 1], weight)
    before = (
        lax.broadcasted_iota(jnp.int32, (n_tok, n_tok), 1) < lax.broadcasted_iota(jnp.int32, (n_tok, n_tok), 0)
    ).astype(jnp.float32)
    slot = matmul(before, named, (1, 0))
    chosen = jnp.where(slot == (r_of % SLOTS).astype(jnp.float32), named, 0.0)
    first = r_of < SLOTS
    plain = jnp.where(first, chosen, 0.0)
    scale = jnp.where(first, 0.0, chosen * weight)
    high = scale.astype(jnp.bfloat16).astype(jnp.float32)
    mid = (scale - high).astype(jnp.bfloat16).astype(jnp.float32)
    route[...] = jnp.concatenate([plain, high, mid, scale - high - mid], axis=0).astype(jnp.bfloat16)

    def place(dim, shape):
        c = lax.broadcasted_iota(jnp.int32, shape, dim)
        r, i, f = c % SLOTS, (c % rows) // SLOTS, c // rows
        to = (f * per + i) * USED + r
        return ((r < USED) & (to == lax.broadcasted_iota(jnp.int32, shape, 1 - dim))).astype(jnp.float32)

    pack[...] = place(1, (packed, CUTS * rows)).astype(jnp.bfloat16)
    unpack[...] = place(0, (CUTS * rows, packed)).astype(jnp.bfloat16)

    tok, cot = tok_ref[...].astype(jnp.float32), cot_ref[...].astype(jnp.float32)
    values = jnp.concatenate([tok, cot, cot, cot], axis=0).astype(jnp.bfloat16)
    sbuf[...] = matmul(route[...], values, (0, 0)).astype(jnp.bfloat16)

    pl.semaphore_wait(barrier, n_dp + 1)

    def exchange(src, dst, send_sem, recv_sem, o, sign):
        for i in range(per):
            at = pl.ds(pl.multiple_of(o * span + i * PAIR, PAIR), PAIR)

            def remote():
                pltpu.make_async_remote_copy(
                    src_ref=src.at[at],
                    dst_ref=dst.at[at],
                    send_sem=send_sem,
                    recv_sem=recv_sem,
                    device_id={"dp": partner(o, i, sign)},
                    device_id_type=MESH,
                ).start()

            if i:
                remote()
            else:

                @pl.when(o == 0)
                def _():
                    pltpu.make_async_copy(src.at[at], dst.at[at], recv_sem).start()

                @pl.when(o != 0)
                def _():
                    remote()

    def wait_rows(ref, first_row, count, sem):
        view = ref.at[pl.ds(first_row, count)]
        pltpu.make_async_copy(view, view, sem).wait()

    def send_in(o):
        exchange(sbuf, inbuf, in_send, in_recv.at[o], o, 1)

    far = (z + half) % n_z
    send_in(far)

    @pl.loop(1, half)
    def _(s):
        send_in((z + half - s) % n_z)
        send_in((z + half + s) % n_z)

    send_in(z)
    for load in loads:
        load.wait()

    def arrived(chunks):
        xs, ds = [], []
        for o in chunks:
            at = pl.multiple_of(o * span, span)
            wait_rows(inbuf, at, span, in_recv.at[o])
            both = inbuf[pl.ds(at, span), :].astype(jnp.float32).reshape(per, 2, SLOTS, -1)
            to = pl.ds(pl.multiple_of(o * rows, rows), rows)
            xs.append(both[:, 0].reshape(rows, -1).astype(jnp.bfloat16))
            ds.append(both[:, 1].reshape(rows, -1).astype(jnp.bfloat16))
            xall[to, :] = xs[-1]
            dall[to, :] = ds[-1]
        xrows = jnp.concatenate(xs, axis=0) if len(xs) > 1 else xs[0]
        drows = jnp.concatenate(ds, axis=0) if len(ds) > 1 else ds[0]
        return xrows, xrows, drows

    def partial(a, chunks, lhs):
        product = matmul(lhs[a], wts[a], (1, 1)).astype(jnp.bfloat16)
        for n, o in enumerate(chunks):
            mine = product[n * rows : (n + 1) * rows]
            stacked = jnp.concatenate(
                [mine[:, f * quarter : (f + 1) * quarter] for f in range(CUTS)], axis=0
            )
            part[o, a * packed : (a + 1) * packed] = matmul(pack[...], stacked, (1, 0)).astype(jnp.bfloat16)

    def partials(chunks):
        lhs = arrived(chunks)
        for a in range(3):
            partial(a, chunks, lhs)

    sides = (z_right, z_left)

    def rs_copy(d, s, o, m, first, count):
        at = pl.ds(first, count)
        return pltpu.make_async_remote_copy(
            src_ref=part.at[o].at[at],
            dst_ref=landed.at[d, s].at[at],
            send_sem=rs_send.at[d, s, m],
            recv_sem=rs_recv.at[d, s, m],
            device_id={"expert": sides[d]},
            device_id_type=MESH,
        )

    def ag_copy(d, s, o, m, first, count):
        at = pl.ds(first, count)
        return pltpu.make_async_remote_copy(
            src_ref=held.at[o].at[at],
            dst_ref=held.at[o].at[at],
            send_sem=ag_send.at[d, s, m],
            recv_sem=ag_recv.at[d, s, m],
            device_id={"expert": sides[d]},
            device_id_type=MESH,
        )

    partials([far])
    for n in range(centre + 1):
        for d in range(2):
            rs_copy(d, 0, far, *far_msgs[d][n]).start()

    def ends(s):
        return (z + half - s) % n_z, (z + half + s) % n_z

    def add_on(d, s, o, m, first, count):
        rs_copy(d, s, o, m, first, count).wait_recv()
        at = pl.ds(first, count)
        part[o, at, :] = (
            part[o, at, :].astype(jnp.float32) + landed[d, s, at, :].astype(jnp.float32)
        ).astype(jnp.bfloat16)

    near = ends(1)
    partials(near)
    for n in range(centre):
        rs_copy(0, 1, near[0], *msgs[centre + 1 + n]).start()
        rs_copy(1, 1, near[1], *msgs[n]).start()
    for n in range(centre + 1):
        for d in range(2):
            add_on(d, 0, near[d], *far_msgs[d][n])
            rs_copy(d, 1, near[d], *msgs[far_msgs[d][n][0]]).start()

    def rs_step(s, following):
        chunks = ends(s)
        lhs = None
        for n in range(PIECES):
            for d in range(2):
                add_on(d, s - 1, chunks[d], *rs_order[d][n])
                rs_copy(d, s, chunks[d], *rs_order[d][n]).start()
            lhs = arrived(following) if n == 0 else lhs
            if n < 3:
                partial(n, following, lhs)

    if half > 2:
        partials(ends(2))

        @pl.loop(2, half - 1)
        def _(s):
            rs_step(s, ends(s + 1))

        rs_step(half - 1, (z,))
    else:
        partials([z])

    def landed_sum(a):
        at = pl.ds(a * packed, packed)
        return (
            part[z, at, :].astype(jnp.float32)
            + landed[0, half - 1, at, :].astype(jnp.float32)
            + landed[1, half - 1, at, :].astype(jnp.float32)
        )

    def hold(a, value):
        held[z, a * packed : (a + 1) * packed] = value.astype(jnp.bfloat16)

    early = [msg for msg in msgs if msg[1] < 2 * packed]
    late = [msg for msg in msgs if msg[1] >= 2 * packed]
    ready = [msg for msg in msgs if msg[1] + msg[2] <= packed]
    for msg in early:
        for d in range(2):
            rs_copy(d, half - 1, z, *msg).wait_recv()
    gate, up = landed_sum(0), landed_sum(1)
    sig = jax.nn.sigmoid(gate)
    active = gate * sig
    hold(0, active * up)
    for msg in ready:
        for d in range(2):
            ag_copy(d, 1, z, *msg).start()
    for msg in late:
        for d in range(2):
            rs_copy(d, half - 1, z, *msg).wait_recv()
    hgrad = landed_sum(2)
    hold(1, hgrad * active)
    hold(2, hgrad * up * sig * (1.0 + gate * (1.0 - sig)))
    for n in range(PIECES):
        for d in range(2):
            if ag_order[d][n] not in ready:
                ag_copy(d, 1, z, *ag_order[d][n]).start()

    def outward(chunks):
        lhs = []
        for a in range(3):
            whole = []
            for o in chunks:
                stacked = matmul(unpack[...], held[o, a * packed : (a + 1) * packed], (1, 0)).astype(jnp.bfloat16)
                whole.append(
                    jnp.concatenate([stacked[f * rows : (f + 1) * rows] for f in range(CUTS)], axis=1)
                )
                hall[a, pl.ds(pl.multiple_of(o * rows, rows), rows), :] = whole[-1]
            lhs.append(jnp.concatenate(whole, axis=0) if len(whole) > 1 else whole[0])
        out = matmul(lhs[0], wts[2], (1, 0))
        back = matmul(lhs[1], wts[1], (1, 0)) + matmul(lhs[2], wts[0], (1, 0))
        for n, o in enumerate(chunks):
            mine = slice(n * rows, (n + 1) * rows)
            both = jnp.stack(
                [back[mine].reshape(per, SLOTS, -1), out[mine].reshape(per, SLOTS, -1)], axis=1
            ).reshape(span, -1)
            obuf[pl.ds(pl.multiple_of(o * span, span), span), :] = both.astype(jnp.bfloat16)
            exchange(obuf, rbuf, out_send, out_recv, o, -1)

    outward([z])

    @pl.loop(1, half - 1)
    def _(s):
        chunks = ((z - s + n_z) % n_z, (z + s) % n_z)
        for n in range(PIECES):
            for d in range(2):
                ag_copy(d, s, chunks[d], *ag_order[d][n]).wait_recv()
                ag_copy(d, s + 1, chunks[d], *ag_order[d][n]).start()
        outward(chunks)

    last = ((z - (half - 1) + n_z) % n_z, (z + half - 1) % n_z)
    for n in range(PIECES):
        for d in range(2):
            ag_copy(d, half - 1, last[d], *ag_order[d][n]).wait_recv()
            for part_msg in far_msgs[d]:
                if part_msg[0] == ag_order[d][n][0]:
                    ag_copy(d, half, last[d], *part_msg).start()
    outward(last)
    for d in range(2):
        for msg in far_msgs[d]:
            ag_copy(d, half, far, *msg).wait_recv()
    outward([far])

    for a in range(3):
        grads[2 - a] = matmul(hall[a], (xall if a else dall)[...], (0, 0)).astype(jnp.bfloat16)

    wait_rows(rbuf, 0, n_z * span, out_recv)
    wait_rows(sbuf, 0, n_z * span - PAIR, in_send)
    wait_rows(obuf, 0, n_z * span - PAIR, out_send)
    for d in range(2):
        for msg in far_msgs[d]:
            rs_copy(d, 0, far, *msg).wait_send()
            ag_copy(d, half, far, *msg).wait_send()

    @pl.loop(1, half)
    def _(s):
        for msg in msgs:
            for d in range(2):
                rs_copy(d, s, z, *msg).wait_send()
                ag_copy(d, s, z, *msg).wait_send()


def finish(route, rbuf, grads, mixed_ref, tgrad_ref, ggrad_hbm, ugrad_hbm, dgrad_hbm, sem):
    stores = [
        pltpu.make_async_copy(grads.at[a], dst.at[0], sem.at[a])
        for a, dst in enumerate((ggrad_hbm, ugrad_hbm, dgrad_hbm))
    ]
    for store in stores:
        store.start()
    n_tok = mixed_ref.shape[0]
    total = matmul(route[...], rbuf[...], (1, 0))
    tgrad_ref[...] = total[:n_tok].astype(jnp.bfloat16)
    mixed_ref[...] = (total[n_tok : 2 * n_tok] + total[2 * n_tok : 3 * n_tok] + total[3 * n_tok :]).astype(
        jnp.bfloat16
    )
    for store in stores:
        store.wait()


def shards(n_z, n_dp, tokens, expert_ids, gate_probs, cotangent, w_gate, w_up, w_down):
    n_tok, feats = tokens.shape
    ff = w_gate.shape[1]
    rows = n_dp // n_z * SLOTS
    both = n_dp * PAIR
    packed = CUTS * (n_dp // n_z) * USED
    half = n_z // 2
    bf16 = jnp.bfloat16
    vmem = pl.BlockSpec(memory_space=pltpu.VMEM)
    anywhere = pl.BlockSpec(memory_space=pltpu.HBM)
    act = jax.ShapeDtypeStruct((n_tok, feats), bf16)
    grad = jax.ShapeDtypeStruct((1, ff, feats), bf16)
    dma = pltpu.SemaphoreType.DMA
    route, rbuf, grads = pl.pallas_call(
        functools.partial(kernel, n_z, n_dp),
        out_shape=(
            pltpu.VMEM((4 * n_tok, both), bf16),
            pltpu.VMEM((both, feats), bf16),
            pltpu.VMEM((3, ff, feats), bf16),
        ),
        in_specs=[anywhere] * 7,
        out_specs=(vmem, vmem, vmem),
        scratch_shapes=[
            pltpu.VMEM(expert_ids.shape[::-1], jnp.int32),
            pltpu.VMEM(expert_ids.shape[::-1], jnp.float32),
            pltpu.VMEM((n_tok, feats), bf16),
            pltpu.VMEM((n_tok, feats), bf16),
            pltpu.VMEM((3, ff, feats), bf16),
            pltpu.VMEM((both, feats), bf16),
            pltpu.VMEM((both, feats), bf16),
            pltpu.VMEM((both, feats), bf16),
            pltpu.VMEM((n_z * rows, feats), bf16),
            pltpu.VMEM((n_z * rows, feats), bf16),
            pltpu.VMEM((packed, CUTS * rows), bf16),
            pltpu.VMEM((CUTS * rows, packed), bf16),
            pltpu.VMEM((n_z, 3 * packed, ff // CUTS), bf16),
            pltpu.VMEM((2, half, 3 * packed, ff // CUTS), bf16),
            pltpu.VMEM((n_z, 3 * packed, ff // CUTS), bf16),
            pltpu.VMEM((3, n_z * rows, ff), bf16),
            dma((3,)),
            dma((4,)),
            dma,
            dma((n_z,)),
            dma,
            dma,
            dma((2, half, PIECES)),
            dma((2, half, PIECES)),
            dma((2, half + 1, PIECES)),
            dma((2, half + 1, PIECES)),
        ],
        compiler_params=pltpu.CompilerParams(
            collective_id=0, has_side_effects=True, vmem_limit_bytes=56 * 1024 * 1024
        ),
        name="experts",
    )(expert_ids.T, gate_probs.T, tokens, cotangent, w_gate, w_up, w_down)
    return pl.pallas_call(
        finish,
        out_shape=(act, act, grad, grad, grad),
        in_specs=[vmem] * 3,
        out_specs=(vmem, vmem, anywhere, anywhere, anywhere),
        scratch_shapes=[dma((3,))],
        compiler_params=pltpu.CompilerParams(vmem_limit_bytes=16 * 1024 * 1024),
        name="finish",
    )(route, rbuf, grads)


def solution(mesh):
    n_z, n_dp = mesh.shape["expert"], mesh.shape["dp"]
    split = P("dp", "expert")
    weight = P("dp", None, "expert")
    return jax.shard_map(
        functools.partial(shards, n_z, n_dp),
        mesh=mesh,
        in_specs=(split, P("dp", None), P("dp", None), split, weight, weight, weight),
        out_specs=(split, split, weight, weight, weight),
        check_vma=False,
    )
```
